32 devices in a mesh: grp: 2 (over y), step: 4 (over z), chain: 2 (over x), rep: 2 (over core).
Axes of the slice: x: 2, y: 2, z: 4, core: 2. Of those that a mesh axis runs over, the one named last changes fastest.
Arguments:
- init_seed: int32 [8], P(('grp', 'chain', 'rep')), parts along dimension 0, may hold values from 0 to 63
- noise_index: int32 [8, 32], P(('grp', 'chain', 'rep'), 'step'), parts along dimension 0, may hold values from 0 to 4095
- init_table: float32 [64, 256], replicated, may hold values from -6 to 6
- noise_table: float32 [4096, 256], replicated, may hold values from -6 to 6
- weight: float32 [256, 256], replicated
- bias: float32 [256], replicated, may hold values from -3 to 3
- rates: float32 [64, 256], P(('grp', 'step')), parts along dimension 0, may hold values from 0 to 0.5
- old_path: float32 [8, 32, 256], P(('grp', 'chain', 'rep'), 'step'), parts along dimension 0, may hold values from -6 to 6
- cotangent: float32 [8, 32, 256], P(('grp', 'chain', 'rep'), 'step'), parts along dimension 0, may hold values from -0.3 to 0.3
Outputs:
- path_new: float32 [8, 32, 256], P(('grp', 'chain', 'rep'), 'step'), parts along dimension 0
- grad_w: float32 [512, 256], P('grp'), parts along dimension 0
- grad_b: float32 [512], P('grp'), parts along dimension 0
The draws below stay inside these ranges and needn't reach their ends.
There are 2 independent parts, one for each index of `grp`. The reference program is written for one: setup_inputs(seed, part) draws one part's arguments, and reference() takes and returns one part's arrays. A program takes and returns all parts, laid end to end along the dimension named above; an argument that names none is the same for every part. Nothing has to cross between parts.
All inputs are finite; a program needn't handle non-finite values.
Results may differ from the reference program's by a relative error of at most 0.0001.
Values sent between devices are 32-bit elements; how exact they have to be, the bound alone decides.
A program may use at most 64 MiB of HBM per device.

```python
import math
import jax
import jax.numpy as jnp
from jax import lax

LATENT_WIDTH = 256
NNOISE = 4096
NSEEDS = 64
SAMPLER_LENGTH = 32
CHAINS = 4


def draw_weight(key, part):
    first_key, second_key = jax.random.split(jax.random.fold_in(key, 11))
    skew_base = jax.random.normal(first_key, (LATENT_WIDTH, LATENT_WIDTH), jnp.float32)
    sym_base = jax.random.normal(second_key, (LATENT_WIDTH, LATENT_WIDTH), jnp.float32)
    return (skew_base - skew_base.T) / math.sqrt(2.0 * LATENT_WIDTH) + 0.05 * sym_base / math.sqrt(1.0 * LATENT_WIDTH)


def draw_rates(key, part):
    seed_handles = jax.random.split(jax.random.fold_in(key, 23), 4)
    low_end = math.log(0.25 / SAMPLER_LENGTH)
    high_end = math.log(1.0 / 30.0)
    starting_operator = jnp.exp(jax.random.uniform(seed_handles[0], (LATENT_WIDTH,), jnp.float32, low_end, high_end))
    multiplier_size = jnp.exp(jax.random.uniform(seed_handles[1], (SAMPLER_LENGTH, LATENT_WIDTH), jnp.float32, math.log(0.5), math.log(1.5)))
    spots = jax.random.randint(seed_handles[2], (3,), 0, SAMPLER_LENGTH)
    success_tally = jnp.any(jnp.arange(SAMPLER_LENGTH)[:, None] == spots[None, :], axis=1)
    grouped_lines = jax.random.uniform(seed_handles[3], (SAMPLER_LENGTH, LATENT_WIDTH), jnp.float32, 0.2, 0.5)
    return jnp.where(success_tally[:, None], grouped_lines, starting_operator[None, :] * multiplier_size)


def plant(values, stream_key, smallest, largest):
    place = [jax.random.randint(jax.random.fold_in(stream_key, axis), (), 0, length) for axis, length in enumerate(values.shape)]
    longest = values.shape.index(max(values.shape))
    neighbour = place[:longest] + [(place[longest] + 1) % values.shape[longest]] + place[longest + 1:]
    return values.at[tuple(place)].set(smallest).at[tuple(neighbour)].set(largest)


def block_levels(key, shape, cuts, smallest, largest):
    def one(position, blocks):
        steps = jax.random.uniform(jax.random.fold_in(jax.random.fold_in(key, 6), position), (blocks,), jnp.float32, smallest / len(cuts), largest / len(cuts))
        return jnp.repeat(jnp.exp(steps), shape[position] // blocks).reshape((-1,) + (1,) * (len(shape) - position - 1))

    gain = one(*cuts[0])
    for cut in cuts[1:]:
        gain = gain * one(*cut)
    return gain


def normal_values(rng, shape, deviation, most, pieces=(), held_as=jnp.bfloat16):
    array = jax.random.normal(rng, shape, jnp.float32) * deviation
    if len(pieces) > 0:
        array = block_levels(rng, shape, pieces, -0.22, 0.18) * array
    return jnp.clip(array, min=-most, max=most).astype(held_as)


def setup_inputs(seed: int = 0, part: int = 0) -> dict:
    keys = jax.random.split(jax.random.key(seed), 10)
    own_keys = jax.random.split(jax.random.fold_in(keys[9], part), 10)
    return {
        "init_seed": plant(jax.random.randint(own_keys[0], (CHAINS,), 0, NSEEDS), jax.random.fold_in(own_keys[0], 1), 0, NSEEDS - 1).astype(jnp.int32),
        "noise_index": plant(jax.random.randint(own_keys[1], (CHAINS, SAMPLER_LENGTH), 0, NNOISE), jax.random.fold_in(own_keys[1], 1), 0, NNOISE - 1).astype(jnp.int32),
        "init_table": normal_values(keys[2], (NSEEDS, LATENT_WIDTH), 1.0, 6.0, (), jnp.float32),
        "noise_table": normal_values(keys[3], (NNOISE, LATENT_WIDTH), 1.0, 6.0, (), jnp.float32),
        "weight": draw_weight(jax.random.fold_in(keys[9], 71), part),
        "bias": normal_values(keys[5], (LATENT_WIDTH,), 0.5, 3.0, (), jnp.float32),
        "rates": draw_rates(jax.random.fold_in(jax.random.fold_in(keys[9], part), 71), part),
        "old_path": normal_values(own_keys[7], (CHAINS, SAMPLER_LENGTH, LATENT_WIDTH), 1.0, 6.0, ((0, 4), (1, 4)), jnp.float32),
        "cotangent": normal_values(own_keys[8], (CHAINS, SAMPLER_LENGTH, LATENT_WIDTH), 0.05, 0.3, ((0, 4), (1, 4)), jnp.float32),
    }


def reference(init_seed, noise_index, init_table, noise_table, weight, bias, rates, old_path, cotangent):
    highest = lax.Precision.HIGHEST
    step_size = 4.0 / SAMPLER_LENGTH
    start_state = init_table[init_seed]
    previous = jnp.concatenate([start_state[:, None], old_path[:, :-1]], axis=1)
    mixed = jnp.einsum("ctj,ij->cti", previous, weight, precision=highest)
    squash = jnp.tanh(mixed + bias + noise_table[noise_index])
    slope = 1.0 - squash * squash
    keep_rate = 1.0 - rates
    offset = step_size * (squash - slope * mixed)
    slope_major = jnp.swapaxes(slope, 0, 1)

    def forward_step(state, inputs):
        keep_now, slope_now, offset_now = inputs
        state = keep_now * state + step_size * slope_now * jnp.dot(state, weight.T, precision=highest) + offset_now
        return state, state

    final_state, path_major = lax.scan(forward_step, start_state, (keep_rate, slope_major, jnp.swapaxes(offset, 0, 1)))
    path_new = jnp.swapaxes(path_major, 0, 1)

    def backward_step(carried, inputs):
        keep_now, slope_now, cot_now = inputs
        adjoint_now = cot_now + carried
        carried = keep_now * adjoint_now + step_size * jnp.dot(slope_now * adjoint_now, weight, precision=highest)
        return carried, adjoint_now

    final_carry, adjoint_major = lax.scan(backward_step, jnp.zeros_like(start_state), (keep_rate, slope_major, jnp.swapaxes(cotangent, 0, 1)), reverse=True)
    adjoint = jnp.swapaxes(adjoint_major, 0, 1)
    weighted = adjoint * slope
    grad_w = step_size * jnp.einsum("cti,ctj->ij", weighted, previous, precision=highest)
    grad_b = step_size * jnp.sum(weighted, axis=(0, 1))
    return (path_new, grad_w, grad_b)
```

```python
import functools

import jax
import jax.numpy as jnp
from jax import lax
from jax.experimental import pallas as pl
from jax.experimental.pallas import tpu as pltpu
from jax.sharding import PartitionSpec as P

F32 = jnp.float32
BF16 = jnp.bfloat16
MESH = pl.DeviceIdType.MESH


def split(x):
    high = x.astype(BF16)
    return high, (x - high.astype(F32)).astype(BF16)


def rows_to_block(rows, steps, width):
    row = lax.broadcasted_iota(jnp.int32, (steps, width), 0)
    block = jnp.zeros((steps, width), F32)
    for t, value in rows.items():
        block = jnp.where(row == t, value, block)
    return block


def kernel(
    sizes, step_size,
    seed_ref, index_ref, init_ref, noise_ref, weight_ref, bias_ref, rates_ref, old_ref, cot_ref,
    path_ref, gw_ref, gb_ref,
    noise_v, maps, off_cols, cot_cols, edge_in, fwd_in, bwd_in, fwd_out, bwd_out,
    all_prev, all_weighted, slope_v,
    noise_sem, edge_send, edge_recv, fwd_send, fwd_recv, bwd_send, bwd_recv,
    prev_send, prev_recv, weighted_send, weighted_recv,
):
    ranks, chains, reps = sizes
    peers = ranks * chains * reps
    steps, width = old_ref.shape
    half = width // 2
    s, c, r = lax.axis_index("step"), lax.axis_index("chain"), lax.axis_index("rep")
    me = (s * chains + c) * reps + r

    def peer(d):
        other = lax.rem(me + d, peers)
        return {
            "step": other // (chains * reps),
            "chain": lax.rem(other // reps, chains),
            "rep": lax.rem(other, reps),
        }

    def each_peer(body):
        if peers <= 32:
            for d in range(1, peers):
                body(d)
        else:
            def one(d, carry):
                body(d)
                return carry
            lax.fori_loop(1, peers, one, 0)

    pieces = noise_sem.shape[0]
    piece = noise_ref.shape[0] // pieces
    loads = [
        pltpu.make_async_copy(
            noise_ref.at[pl.ds(k * piece, piece)], noise_v.at[pl.ds(k * piece, piece)], noise_sem.at[k]
        )
        for k in range(pieces)
    ]
    for load in loads:
        load.start()

    barrier = pltpu.get_barrier_semaphore()
    each_peer(
        lambda d: pl.semaphore_signal(barrier, inc=1, device_id=peer(d), device_id_type=MESH)
    )

    weight = weight_ref[...]
    weight_t = weight.T
    w_high, w_low = split(weight_t)
    pl.semaphore_wait(barrier, peers - 1)

    edge = pltpu.make_async_remote_copy(
        src_ref=old_ref.at[pl.ds(steps - 1, 1)], dst_ref=edge_in, send_sem=edge_send,
        recv_sem=edge_recv, device_id={"step": lax.rem(s + 1, ranks)}, device_id_type=MESH,
    )

    @pl.when(s < ranks - 1)
    def _():
        edge.start()

    start = init_ref[pl.ds(seed_ref[0], 1), :]
    for load in loads:
        load.wait()
    row = lax.broadcasted_iota(jnp.int32, (steps, width), 0)
    noise = jnp.concatenate([noise_v[pl.ds(index_ref[0, t], 1), :] for t in range(steps)], 0)

    @pl.when(s > 0)
    def _():
        edge.wait_recv()

    @pl.when(s == 0)
    def _():
        edge_in[...] = start

    first = edge_in[...]
    previous = jnp.concatenate([first, old_ref[0 : steps - 1, :]], 0)
    all_prev[0] = previous

    def prev_copy(d):
        return pltpu.make_async_remote_copy(
            src_ref=all_prev.at[0], dst_ref=all_prev.at[d], send_sem=prev_send.at[d],
            recv_sem=prev_recv.at[d], device_id=peer(d), device_id_type=MESH,
        )

    def weighted_copy(d):
        return pltpu.make_async_remote_copy(
            src_ref=all_weighted.at[0], dst_ref=all_weighted.at[d], send_sem=weighted_send.at[d],
            recv_sem=weighted_recv.at[d], device_id=peer(d), device_id_type=MESH,
        )

    def dot(a, b):
        return jnp.dot(a, b, preferred_element_type=F32)

    p_high, p_low = split(previous)
    mixed = dot(p_high, w_high) + (dot(p_low, w_high) + dot(p_high, w_low))
    squash = jnp.tanh(mixed + bias_ref[...] + noise)
    slope = 1.0 - squash * squash
    slope_v[...] = slope
    offset = step_size * (squash - slope * mixed)
    scaled = step_size * slope
    keep = 1.0 - rates_ref[...]
    cot = cot_ref[...]
    stacked = jnp.concatenate([scaled, offset, cot, jnp.zeros((128 - 3 * steps, width), F32)], 0)
    columns = stacked.T
    lane = lax.broadcasted_iota(jnp.int32, (width, 128), 1)
    diagonal = lax.broadcasted_iota(jnp.int32, (width, width), 0) == lax.broadcasted_iota(
        jnp.int32, (width, width), 1
    )
    for t in range(steps):
        kept = jnp.where(diagonal, keep[t : t + 1], 0.0)
        if t % 2 == 0:
            maps[t] = weight * columns[:, t : t + 1] + kept
            off_cols[t // 2] = jnp.where(lane == steps + t, columns, 0.0)
            cot_cols[t // 2] = jnp.where(lane == 2 * steps + t, columns, 0.0)
        else:
            maps[t] = weight_t * scaled[t : t + 1] + kept

    def to_column(t, x, extra):
        part = maps[t, :, :half] * x[:, :half] + maps[t, :, half:] * x[:, half:]
        return jnp.sum(part + extra, axis=1, keepdims=True)

    def to_row(t, x):
        return jnp.sum(maps[t] * x, axis=0, keepdims=True)

    def gather_columns(cols):
        total = jnp.zeros((width, 128), F32)
        for t, value in cols.items():
            total = jnp.where(lane == t, value, total)
        return total.T[0:steps]

    forward = pltpu.make_async_remote_copy(
        src_ref=fwd_out, dst_ref=fwd_in, send_sem=fwd_send, recv_sem=fwd_recv,
        device_id={"step": lax.rem(s + 1, ranks)}, device_id_type=MESH,
    )
    backward = pltpu.make_async_remote_copy(
        src_ref=bwd_out, dst_ref=bwd_in, send_sem=bwd_send, recv_sem=bwd_recv,
        device_id={"step": lax.rem(s + ranks - 1, ranks)}, device_id_type=MESH,
    )

    def run_forward():
        @pl.when(s == 0)
        def _():
            fwd_in[...] = start

        @pl.when(s > 0)
        def _():
            forward.wait_recv()

        x = fwd_in[...]
        rows, cols = {}, {}
        for t in range(steps):
            if t % 2 == 0:
                x = to_column(t, x, off_cols[t // 2])
                cols[t] = x
            else:
                x = to_row(t, x) + offset[t : t + 1]
                rows[t] = x
        fwd_out[...] = x

        @pl.when(s < ranks - 1)
        def _():
            forward.start()

        path_ref[...] = jnp.where(
            row % 2 == 0, gather_columns(cols), rows_to_block(rows, steps, width)
        )

    def run_backward():
        @pl.when(s == ranks - 1)
        def _():
            bwd_in[...] = jnp.zeros((1, width), F32)

        @pl.when(s < ranks - 1)
        def _():
            backward.wait_recv()

        a = bwd_in[...] + cot[steps - 1 : steps]
        rows, cols = {steps - 1: a}, {}
        for t in range(steps - 1, 0, -1):
            if t % 2 == 1:
                a = to_column(t, a, cot_cols[(t - 1) // 2])
                cols[t - 1] = a
            else:
                a = to_row(t, a) + cot[t - 1 : t]
                rows[t - 1] = a
        bwd_out[...] = to_row(0, a)

        @pl.when(s > 0)
        def _():
            backward.start()

        adjoint = jnp.where(
            row % 2 == 0, gather_columns(cols), rows_to_block(rows, steps, width)
        )
        all_weighted[0] = adjoint * slope_v[...]
        each_peer(lambda d: weighted_copy(d).start())

    early = s < ranks // 2

    @pl.when(early)
    def _():
        run_forward()
        each_peer(lambda d: prev_copy(d).start())
        run_backward()

    @pl.when(jnp.logical_not(early))
    def _():
        run_backward()
        each_peer(lambda d: prev_copy(d).start())
        run_forward()

    each_peer(lambda d: prev_copy(d).wait_recv())
    left = all_prev[...].reshape(peers * steps, width)
    l_high, l_low = split(left)
    each_peer(lambda d: weighted_copy(d).wait_recv())
    total = all_weighted[...].reshape(peers * steps, width)
    t_high, t_low = split(total)
    dims = (((0,), (0,)), ((), ()))

    def outer(a, b):
        return lax.dot_general(a, b, dims, preferred_element_type=F32)

    gw_ref[...] = step_size * (
        outer(t_high, l_high) + (outer(t_low, l_high) + outer(t_high, l_low))
    )
    gb_ref[...] = step_size * jnp.sum(total, axis=0, keepdims=True)

    each_peer(lambda d: prev_copy(d).wait_send())
    each_peer(lambda d: weighted_copy(d).wait_send())

    @pl.when(s < ranks - 1)
    def _():
        edge.wait_send()
        forward.wait_send()

    @pl.when(s > 0)
    def _():
        backward.wait_send()


def shards(sizes, seed, index, init_table, noise_table, weight, bias, rates, old_path, cotangent):
    ranks, chains, reps = sizes
    peers = ranks * chains * reps
    _, steps, width = old_path.shape
    vmem = pl.BlockSpec(memory_space=pltpu.VMEM)
    smem = pl.BlockSpec(memory_space=pltpu.SMEM)
    dma = pltpu.SemaphoreType.DMA
    path, grad_w, grad_b = pl.pallas_call(
        functools.partial(kernel, sizes, 4.0 / (steps * ranks)),
        out_shape=(
            jax.ShapeDtypeStruct((steps, width), F32),
            jax.ShapeDtypeStruct((width, width), F32),
            jax.ShapeDtypeStruct((1, width), F32),
        ),
        in_specs=[smem, smem, vmem, pl.BlockSpec(memory_space=pl.ANY)] + [vmem] * 5,
        out_specs=(vmem, vmem, vmem),
        scratch_shapes=[
            pltpu.VMEM(noise_table.shape, F32),
            pltpu.VMEM((steps, width, width), F32),
            pltpu.VMEM((steps // 2, width, 128), F32),
            pltpu.VMEM((steps // 2, width, 128), F32),
            pltpu.VMEM((1, width), F32),
            pltpu.VMEM((1, width), F32),
            pltpu.VMEM((1, width), F32),
            pltpu.VMEM((1, width), F32),
            pltpu.VMEM((1, width), F32),
            pltpu.VMEM((peers, steps, width), F32),
            pltpu.VMEM((peers, steps, width), F32),
            pltpu.VMEM((steps, width), F32),
            dma((8,)),
            dma, dma, dma, dma, dma, dma,
            dma((peers,)), dma((peers,)), dma((peers,)), dma((peers,)),
        ],
        compiler_params=pltpu.CompilerParams(
            collective_id=0, has_side_effects=True, vmem_limit_bytes=40 * 1024 * 1024
        ),
    )(
        seed, index, init_table, noise_table, weight, bias.reshape(1, width), rates,
        old_path.reshape(steps, width), cotangent.reshape(steps, width),
    )
    return path.reshape(1, steps, width), grad_w, grad_b.reshape(width)


def solution(mesh):
    sizes = (mesh.shape["step"], mesh.shape["chain"], mesh.shape["rep"])
    across = ("grp", "chain", "rep")
    placed = (
        P(across), P(across, "step"), P(), P(), P(), P(), P(("grp", "step"), None),
        P(across, "step", None), P(across, "step", None),
    )
    return jax.shard_map(
        functools.partial(shards, sizes),
        mesh=mesh,
        in_specs=placed,
        out_specs=(P(across, "step", None), P("grp", None), P("grp")),
        check_vma=False,
    )
```

```python
import functools

import jax
import jax.numpy as jnp
from jax import lax
from jax.experimental import pallas as pl
from jax.experimental.pallas import tpu as pltpu
from jax.sharding import PartitionSpec as P

F32 = jnp.float32
BF16 = jnp.bfloat16
MESH = pl.DeviceIdType.MESH


def split(x):
    high = x.astype(BF16)
    return high, (x - high.astype(F32)).astype(BF16)


def rows_to_block(rows, steps, width):
    row = lax.broadcasted_iota(jnp.int32, (steps, width), 0)
    block = jnp.zeros((steps, width), F32)
    for t, value in rows.items():
        block = jnp.where(row == t, value, block)
    return block


def kernel(
    sizes, step_size,
    seed_ref, index_ref, init_hbm, noise_ref, weight_hbm, bias_hbm, rates_hbm, old_hbm, cot_hbm,
    path_ref, gw_ref, gb_ref,
    init_ref, weight_ref, bias_ref, rates_ref, old_ref, cot_ref, input_sem,
    noise_v, maps, off_cols, cot_cols, edge_in, fwd_in, bwd_in, fwd_out, bwd_out,
    all_prev, all_weighted, slope_v,
    noise_sem, edge_send, edge_recv, fwd_send, fwd_recv, bwd_send, bwd_recv,
    prev_send, prev_recv, weighted_send, weighted_recv,
):
    ranks, chains, reps = sizes
    peers = ranks * chains * reps
    steps, width = old_ref.shape
    half = width // 2
    s, c, r = lax.axis_index("step"), lax.axis_index("chain"), lax.axis_index("rep")
    me = (s * chains + c) * reps + r

    def peer(d):
        other = lax.rem(me + d, peers)
        return {
            "step": other // (chains * reps),
            "chain": lax.rem(other // reps, chains),
            "rep": lax.rem(other, reps),
        }

    def each_peer(body):
        if peers <= 32:
            for d in range(1, peers):
                body(d)
        else:
            def one(d, carry):
                body(d)
                return carry
            lax.fori_loop(1, peers, one, 0)

    inputs = [
        pltpu.make_async_copy(source, target, input_sem.at[k])
        for k, (source, target) in enumerate((
            (weight_hbm, weight_ref), (old_hbm, old_ref), (init_hbm, init_ref),
            (bias_hbm, bias_ref), (rates_hbm, rates_ref), (cot_hbm, cot_ref),
        ))
    ]
    for load in inputs:
        load.start()
    pieces = noise_sem.shape[0]
    piece = noise_ref.shape[0] // pieces
    loads = [
        pltpu.make_async_copy(
            noise_ref.at[pl.ds(k * piece, piece)], noise_v.at[pl.ds(k * piece, piece)], noise_sem.at[k]
        )
        for k in range(pieces)
    ]
    for load in loads:
        load.start()

    barrier = pltpu.get_barrier_semaphore()
    each_peer(
        lambda d: pl.semaphore_signal(barrier, inc=1, device_id=peer(d), device_id_type=MESH)
    )

    for load in inputs:
        load.wait()
    weight = weight_ref[...]
    weight_t = weight.T
    w_high, w_low = split(weight_t)
    pl.semaphore_wait(barrier, peers - 1)

    edge = pltpu.make_async_remote_copy(
        src_ref=old_ref.at[pl.ds(steps - 1, 1)], dst_ref=edge_in, send_sem=edge_send,
        recv_sem=edge_recv, device_id={"step": lax.rem(s + 1, ranks)}, device_id_type=MESH,
    )

    @pl.when(s < ranks - 1)
    def _():
        edge.start()

    start = init_ref[pl.ds(seed_ref[0], 1), :]
    for load in loads:
        load.wait()
    row = lax.broadcasted_iota(jnp.int32, (steps, width), 0)
    noise = jnp.concatenate([noise_v[pl.ds(index_ref[0, t], 1), :] for t in range(steps)], 0)

    @pl.when(s > 0)
    def _():
        edge.wait_recv()

    @pl.when(s == 0)
    def _():
        edge_in[...] = start

    first = edge_in[...]
    previous = jnp.concatenate([first, old_ref[0 : steps - 1, :]], 0)
    all_prev[0] = previous

    def prev_copy(d):
        return pltpu.make_async_remote_copy(
            src_ref=all_prev.at[0], dst_ref=all_prev.at[d], send_sem=prev_send.at[d],
            recv_sem=prev_recv.at[d], device_id=peer(d), device_id_type=MESH,
        )

    def weighted_copy(d):
        return pltpu.make_async_remote_copy(
            src_ref=all_weighted.at[0], dst_ref=all_weighted.at[d], send_sem=weighted_send.at[d],
            recv_sem=weighted_recv.at[d], device_id=peer(d), device_id_type=MESH,
        )

    def dot(a, b):
        return jnp.dot(a, b, preferred_element_type=F32)

    p_high, p_low = split(previous)
    mixed = dot(p_high, w_high) + (dot(p_low, w_high) + dot(p_high, w_low))
    squash = jnp.tanh(mixed + bias_ref[...] + noise)
    slope = 1.0 - squash * squash
    slope_v[...] = slope
    offset = step_size * (squash - slope * mixed)
    scaled = step_size * slope
    keep = 1.0 - rates_ref[...]
    cot = cot_ref[...]
    stacked = jnp.concatenate([scaled, offset, cot, jnp.zeros((128 - 3 * steps, width), F32)], 0)
    columns = stacked.T
    lane = lax.broadcasted_iota(jnp.int32, (width, 128), 1)
    diagonal = lax.broadcasted_iota(jnp.int32, (width, width), 0) == lax.broadcasted_iota(
        jnp.int32, (width, width), 1
    )
    for t in range(steps):
        kept = jnp.where(diagonal, keep[t : t + 1], 0.0)
        if t % 2 == 0:
            maps[t] = weight * columns[:, t : t + 1] + kept
            off_cols[t // 2] = jnp.where(lane == steps + t, columns, 0.0)
            cot_cols[t // 2] = jnp.where(lane == 2 * steps + t, columns, 0.0)
        else:
            maps[t] = weight_t * scaled[t : t + 1] + kept

    def to_column(t, x, extra):
        part = maps[t, :, :half] * x[:, :half] + maps[t, :, half:] * x[:, half:]
        return jnp.sum(part + extra, axis=1, keepdims=True)

    def to_row(t, x):
        return jnp.sum(maps[t] * x, axis=0, keepdims=True)

    def gather_columns(cols):
        total = jnp.zeros((width, 128), F32)
        for t, value in cols.items():
            total = jnp.where(lane == t, value, total)
        return total.T[0:steps]

    forward = pltpu.make_async_remote_copy(
        src_ref=fwd_out, dst_ref=fwd_in, send_sem=fwd_send, recv_sem=fwd_recv,
        device_id={"step": lax.rem(s + 1, ranks)}, device_id_type=MESH,
    )
    backward = pltpu.make_async_remote_copy(
        src_ref=bwd_out, dst_ref=bwd_in, send_sem=bwd_send, recv_sem=bwd_recv,
        device_id={"step": lax.rem(s + ranks - 1, ranks)}, device_id_type=MESH,
    )

    def run_forward():
        @pl.when(s == 0)
        def _():
            fwd_in[...] = start

        @pl.when(s > 0)
        def _():
            forward.wait_recv()

        x = fwd_in[...]
        rows, cols = {}, {}
        for t in range(steps):
            if t % 2 == 0:
                x = to_column(t, x, off_cols[t // 2])
                cols[t] = x
            else:
                x = to_row(t, x) + offset[t : t + 1]
                rows[t] = x
        fwd_out[...] = x

        @pl.when(s < ranks - 1)
        def _():
            forward.start()

        path_ref[...] = jnp.where(
            row % 2 == 0, gather_columns(cols), rows_to_block(rows, steps, width)
        )

    def run_backward():
        @pl.when(s == ranks - 1)
        def _():
            bwd_in[...] = jnp.zeros((1, width), F32)

        @pl.when(s < ranks - 1)
        def _():
            backward.wait_recv()

        a = bwd_in[...] + cot[steps - 1 : steps]
        rows, cols = {steps - 1: a}, {}
        for t in range(steps - 1, 0, -1):
            if t % 2 == 1:
                a = to_column(t, a, cot_cols[(t - 1) // 2])
                cols[t - 1] = a
            else:
                a = to_row(t, a) + cot[t - 1 : t]
                rows[t - 1] = a
        bwd_out[...] = to_row(0, a)

        @pl.when(s > 0)
        def _():
            backward.start()

        adjoint = jnp.where(
            row % 2 == 0, gather_columns(cols), rows_to_block(rows, steps, width)
        )
        all_weighted[0] = adjoint * slope_v[...]
        each_peer(lambda d: weighted_copy(d).start())

    early = s < ranks // 2

    @pl.when(early)
    def _():
        run_forward()
        each_peer(lambda d: prev_copy(d).start())
        run_backward()

    @pl.when(jnp.logical_not(early))
    def _():
        run_backward()
        each_peer(lambda d: prev_copy(d).start())
        run_forward()

    each_peer(lambda d: prev_copy(d).wait_recv())
    left = all_prev[...].reshape(peers * steps, width)
    l_high, l_low = split(left)
    each_peer(lambda d: weighted_copy(d).wait_recv())
    total = all_weighted[...].reshape(peers * steps, width)
    t_high, t_low = split(total)
    dims = (((0,), (0,)), ((), ()))

    def outer(a, b):
        return lax.dot_general(a, b, dims, preferred_element_type=F32)

    gw_ref[...] = step_size * (
        outer(t_high, l_high) + (outer(t_low, l_high) + outer(t_high, l_low))
    )
    gb_ref[...] = step_size * jnp.sum(total, axis=0, keepdims=True)

    each_peer(lambda d: prev_copy(d).wait_send())
    each_peer(lambda d: weighted_copy(d).wait_send())

    @pl.when(s < ranks - 1)
    def _():
        edge.wait_send()
        forward.wait_send()

    @pl.when(s > 0)
    def _():
        backward.wait_send()


def shards(sizes, seed, index, init_table, noise_table, weight, bias, rates, old_path, cotangent):
    ranks, chains, reps = sizes
    peers = ranks * chains * reps
    _, steps, width = old_path.shape
    vmem = pl.BlockSpec(memory_space=pltpu.VMEM)
    smem = pl.BlockSpec(memory_space=pltpu.SMEM)
    dma = pltpu.SemaphoreType.DMA
    path, grad_w, grad_b = pl.pallas_call(
        functools.partial(kernel, sizes, 4.0 / (steps * ranks)),
        out_shape=(
            jax.ShapeDtypeStruct((steps, width), F32),
            jax.ShapeDtypeStruct((width, width), F32),
            jax.ShapeDtypeStruct((1, width), F32),
        ),
        in_specs=[smem, smem] + [pl.BlockSpec(memory_space=pltpu.HBM)] * 7,
        out_specs=(vmem, vmem, vmem),
        scratch_shapes=[
            pltpu.VMEM(init_table.shape, F32),
            pltpu.VMEM(weight.shape, F32),
            pltpu.VMEM((1, width), F32),
            pltpu.VMEM(rates.shape, F32),
            pltpu.VMEM((steps, width), F32),
            pltpu.VMEM((steps, width), F32),
            dma((6,)),
            pltpu.VMEM(noise_table.shape, F32),
            pltpu.VMEM((steps, width, width), F32),
            pltpu.VMEM((steps // 2, width, 128), F32),
            pltpu.VMEM((steps // 2, width, 128), F32),
            pltpu.VMEM((1, width), F32),
            pltpu.VMEM((1, width), F32),
            pltpu.VMEM((1, width), F32),
            pltpu.VMEM((1, width), F32),
            pltpu.VMEM((1, width), F32),
            pltpu.VMEM((peers, steps, width), F32),
            pltpu.VMEM((peers, steps, width), F32),
            pltpu.VMEM((steps, width), F32),
            dma((8,)),
            dma, dma, dma, dma, dma, dma,
            dma((peers,)), dma((peers,)), dma((peers,)), dma((peers,)),
        ],
        compiler_params=pltpu.CompilerParams(
            collective_id=0, has_side_effects=True, vmem_limit_bytes=64 * 1024 * 1024 - 4096
        ),
    )(
        seed, index, init_table, noise_table, weight, bias.reshape(1, width), rates,
        old_path.reshape(steps, width), cotangent.reshape(steps, width),
    )
    return path.reshape(1, steps, width), grad_w, grad_b.reshape(width)


def solution(mesh):
    sizes = (mesh.shape["step"], mesh.shape["chain"], mesh.shape["rep"])
    across = ("grp", "chain", "rep")
    placed = (
        P(across), P(across, "step"), P(), P(), P(), P(), P(("grp", "step"), None),
        P(across, "step", None), P(across, "step", None),
    )
    return jax.shard_map(
        functools.partial(shards, sizes),
        mesh=mesh,
        in_specs=placed,
        out_specs=(P(across, "step", None), P("grp", None), P("grp")),
        check_vma=False,
    )
```

```python
import functools

import jax
import jax.numpy as jnp
from jax import lax
from jax.experimental import pallas as pl
from jax.experimental.pallas import tpu as pltpu
from jax.sharding import PartitionSpec as P

F32 = jnp.float32
BF16 = jnp.bfloat16
MESH = pl.DeviceIdType.MESH


def split(x):
    high = x.astype(BF16)
    return high, (x - high.astype(F32)).astype(BF16)


def rows_to_block(rows, steps, width):
    row = lax.broadcasted_iota(jnp.int32, (steps, width), 0)
    block = jnp.zeros((steps, width), F32)
    for t, value in rows.items():
        block = jnp.where(row == t, value, block)
    return block


def kernel(
    sizes, step_size,
    seed_ref, index_ref, init_hbm, noise_ref, weight_hbm, bias_hbm, rates_hbm, old_hbm, cot_hbm,
    path_ref, gw_ref, gb_ref,
    init_ref, weight_ref, bias_ref, rates_ref, old_ref, cot_ref, input_sem,
    noise_v, maps, off_cols, cot_cols, edge_in, fwd_in, bwd_in, fwd_out, bwd_out,
    all_prev, all_weighted, slope_v,
    noise_sem, edge_send, edge_recv, fwd_send, fwd_recv, bwd_send, bwd_recv,
    prev_send, prev_recv, weighted_send, weighted_recv,
):
    ranks, chains, reps = sizes
    peers = ranks * chains * reps
    steps, width = old_ref.shape
    half = width // 2
    s, c, r = lax.axis_index("step"), lax.axis_index("chain"), lax.axis_index("rep")
    me = (s * chains + c) * reps + r

    def peer(d):
        other = lax.rem(me + d, peers)
        return {
            "step": other // (chains * reps),
            "chain": lax.rem(other // reps, chains),
            "rep": lax.rem(other, reps),
        }

    def each_peer(body):
        if peers <= 32:
            for d in range(1, peers):
                body(d)
        else:
            def one(d, carry):
                body(d)
                return carry
            lax.fori_loop(1, peers, one, 0)

    inputs = [
        pltpu.make_async_copy(source, target, input_sem.at[k])
        for k, (source, target) in enumerate((
            (weight_hbm, weight_ref), (old_hbm, old_ref), (init_hbm, init_ref),
            (bias_hbm, bias_ref), (rates_hbm, rates_ref), (cot_hbm, cot_ref),
        ))
    ]
    for load in inputs:
        load.start()
    pieces = noise_sem.shape[0]
    piece = noise_ref.shape[0] // pieces
    loads = [
        pltpu.make_async_copy(
            noise_ref.at[pl.ds(k * piece, piece)], noise_v.at[pl.ds(k * piece, piece)], noise_sem.at[k]
        )
        for k in range(pieces)
    ]
    for load in loads:
        load.start()

    barrier = pltpu.get_barrier_semaphore()
    each_peer(
        lambda d: pl.semaphore_signal(barrier, inc=1, device_id=peer(d), device_id_type=MESH)
    )

    for load in inputs:
        load.wait()
    weight = weight_ref[...]
    weight_t = weight.T
    w_high, w_low = split(weight_t)
    pl.semaphore_wait(barrier, peers - 1)

    edge = pltpu.make_async_remote_copy(
        src_ref=old_ref.at[pl.ds(steps - 1, 1)], dst_ref=edge_in, send_sem=edge_send,
        recv_sem=edge_recv, device_id={"step": lax.rem(s + 1, ranks)}, device_id_type=MESH,
    )

    @pl.when(s < ranks - 1)
    def _():
        edge.start()

    start = init_ref[pl.ds(seed_ref[0], 1), :]
    for load in loads:
        load.wait()
    row = lax.broadcasted_iota(jnp.int32, (steps, width), 0)
    noise = jnp.concatenate([noise_v[pl.ds(index_ref[0, t], 1), :] for t in range(steps)], 0)

    @pl.when(s > 0)
    def _():
        edge.wait_recv()

    @pl.when(s == 0)
    def _():
        edge_in[...] = start

    first = edge_in[...]
    previous = jnp.concatenate([first, old_ref[0 : steps - 1, :]], 0)
    all_prev[0] = previous

    def prev_copy(d):
        return pltpu.make_async_remote_copy(
            src_ref=all_prev.at[0], dst_ref=all_prev.at[d], send_sem=prev_send.at[d],
            recv_sem=prev_recv.at[d], device_id=peer(d), device_id_type=MESH,
        )

    each_peer(lambda d: prev_copy(d).start())

    def weighted_copy(d):
        return pltpu.make_async_remote_copy(
            src_ref=all_weighted.at[0], dst_ref=all_weighted.at[d], send_sem=weighted_send.at[d],
            recv_sem=weighted_recv.at[d], device_id=peer(d), device_id_type=MESH,
        )

    def dot(a, b):
        return jnp.dot(a, b, preferred_element_type=F32)

    p_high, p_low = split(previous)
    mixed = dot(p_high, w_high) + (dot(p_low, w_high) + dot(p_high, w_low))
    squash = jnp.tanh(mixed + bias_ref[...] + noise)
    slope = 1.0 - squash * squash
    slope_v[...] = slope
    offset = step_size * (squash - slope * mixed)
    scaled = step_size * slope
    keep = 1.0 - rates_ref[...]
    cot = cot_ref[...]
    stacked = jnp.concatenate([scaled, offset, cot, jnp.zeros((128 - 3 * steps, width), F32)], 0)
    columns = stacked.T
    lane = lax.broadcasted_iota(jnp.int32, (width, 128), 1)
    diagonal = lax.broadcasted_iota(jnp.int32, (width, width), 0) == lax.broadcasted_iota(
        jnp.int32, (width, width), 1
    )
    for t in range(steps):
        kept = jnp.where(diagonal, keep[t : t + 1], 0.0)
        if t % 2 == 0:
            maps[t] = weight * columns[:, t : t + 1] + kept
            off_cols[t // 2] = jnp.where(lane == steps + t, columns, 0.0)
            cot_cols[t // 2] = jnp.where(lane == 2 * steps + t, columns, 0.0)
        else:
            maps[t] = weight_t * scaled[t : t + 1] + kept

    def to_column(t, x, extra):
        part = maps[t, :, :half] * x[:, :half] + maps[t, :, half:] * x[:, half:]
        return jnp.sum(part + extra, axis=1, keepdims=True)

    def to_row(t, x):
        return jnp.sum(maps[t] * x, axis=0, keepdims=True)

    def gather_columns(cols):
        total = jnp.zeros((width, 128), F32)
        for t, value in cols.items():
            total = jnp.where(lane == t, value, total)
        return total.T[0:steps]

    forward = pltpu.make_async_remote_copy(
        src_ref=fwd_out, dst_ref=fwd_in, send_sem=fwd_send, recv_sem=fwd_recv,
        device_id={"step": lax.rem(s + 1, ranks)}, device_id_type=MESH,
    )
    backward = pltpu.make_async_remote_copy(
        src_ref=bwd_out, dst_ref=bwd_in, send_sem=bwd_send, recv_sem=bwd_recv,
        device_id={"step": lax.rem(s + ranks - 1, ranks)}, device_id_type=MESH,
    )

    def run_forward():
        @pl.when(s == 0)
        def _():
            fwd_in[...] = start

        @pl.when(s > 0)
        def _():
            forward.wait_recv()

        x = fwd_in[...]
        rows, cols = {}, {}
        for t in range(steps):
            if t % 2 == 0:
                x = to_column(t, x, off_cols[t // 2])
                cols[t] = x
            else:
                x = to_row(t, x) + offset[t : t + 1]
                rows[t] = x
        fwd_out[...] = x

        @pl.when(s < ranks - 1)
        def _():
            forward.start()

        path_ref[...] = jnp.where(
            row % 2 == 0, gather_columns(cols), rows_to_block(rows, steps, width)
        )

    def run_backward():
        @pl.when(s == ranks - 1)
        def _():
            bwd_in[...] = jnp.zeros((1, width), F32)

        @pl.when(s < ranks - 1)
        def _():
            backward.wait_recv()

        a = bwd_in[...] + cot[steps - 1 : steps]
        rows, cols = {steps - 1: a}, {}
        for t in range(steps - 1, 0, -1):
            if t % 2 == 1:
                a = to_column(t, a, cot_cols[(t - 1) // 2])
                cols[t - 1] = a
            else:
                a = to_row(t, a) + cot[t - 1 : t]
                rows[t - 1] = a
        bwd_out[...] = to_row(0, a)

        @pl.when(s > 0)
        def _():
            backward.start()

        adjoint = jnp.where(
            row % 2 == 0, gather_columns(cols), rows_to_block(rows, steps, width)
        )
        all_weighted[0] = adjoint * slope_v[...]
        each_peer(lambda d: weighted_copy(d).start())

    early = s < ranks // 2

    @pl.when(early)
    def _():
        run_forward()
        run_backward()

    @pl.when(jnp.logical_not(early))
    def _():
        run_backward()
        run_forward()

    each_peer(lambda d: prev_copy(d).wait_recv())
    left = all_prev[...].reshape(peers * steps, width)
    l_high, l_low = split(left)
    each_peer(lambda d: weighted_copy(d).wait_recv())
    total = all_weighted[...].reshape(peers * steps, width)
    t_high, t_low = split(total)
    dims = (((0,), (0,)), ((), ()))

    def outer(a, b):
        return lax.dot_general(a, b, dims, preferred_element_type=F32)

    gw_ref[...] = step_size * (
        outer(t_high, l_high) + (outer(t_low, l_high) + outer(t_high, l_low))
    )
    gb_ref[...] = step_size * jnp.sum(total, axis=0, keepdims=True)

    each_peer(lambda d: prev_copy(d).wait_send())
    each_peer(lambda d: weighted_copy(d).wait_send())

    @pl.when(s < ranks - 1)
    def _():
        edge.wait_send()
        forward.wait_send()

    @pl.when(s > 0)
    def _():
        backward.wait_send()


def shards(sizes, seed, index, init_table, noise_table, weight, bias, rates, old_path, cotangent):
    ranks, chains, reps = sizes
    peers = ranks * chains * reps
    _, steps, width = old_path.shape
    vmem = pl.BlockSpec(memory_space=pltpu.VMEM)
    smem = pl.BlockSpec(memory_space=pltpu.SMEM)
    dma = pltpu.SemaphoreType.DMA
    path, grad_w, grad_b = pl.pallas_call(
        functools.partial(kernel, sizes, 4.0 / (steps * ranks)),
        out_shape=(
            jax.ShapeDtypeStruct((steps, width), F32),
            jax.ShapeDtypeStruct((width, width), F32),
            jax.ShapeDtypeStruct((1, width), F32),
        ),
        in_specs=[smem, smem] + [pl.BlockSpec(memory_space=pltpu.HBM)] * 7,
        out_specs=(vmem, vmem, vmem),
        scratch_shapes=[
            pltpu.VMEM(init_table.shape, F32),
            pltpu.VMEM(weight.shape, F32),
            pltpu.VMEM((1, width), F32),
            pltpu.VMEM(rates.shape, F32),
            pltpu.VMEM((steps, width), F32),
            pltpu.VMEM((steps, width), F32),
            dma((6,)),
            pltpu.VMEM(noise_table.shape, F32),
            pltpu.VMEM((steps, width, width), F32),
            pltpu.VMEM((steps // 2, width, 128), F32),
            pltpu.VMEM((steps // 2, width, 128), F32),
            pltpu.VMEM((1, width), F32),
            pltpu.VMEM((1, width), F32),
            pltpu.VMEM((1, width), F32),
            pltpu.VMEM((1, width), F32),
            pltpu.VMEM((1, width), F32),
            pltpu.VMEM((peers, steps, width), F32),
            pltpu.VMEM((peers, steps, width), F32),
            pltpu.VMEM((steps, width), F32),
            dma((8,)),
            dma, dma, dma, dma, dma, dma,
            dma((peers,)), dma((peers,)), dma((peers,)), dma((peers,)),
        ],
        compiler_params=pltpu.CompilerParams(
            collective_id=0, has_side_effects=True, vmem_limit_bytes=64 * 1024 * 1024 - 4096
        ),
    )(
        seed, index, init_table, noise_table, weight, bias.reshape(1, width), rates,
        old_path.reshape(steps, width), cotangent.reshape(steps, width),
    )
    return path.reshape(1, steps, width), grad_w, grad_b.reshape(width)


def solution(mesh):
    sizes = (mesh.shape["step"], mesh.shape["chain"], mesh.shape["rep"])
    across = ("grp", "chain", "rep")
    placed = (
        P(across), P(across, "step"), P(), P(), P(), P(), P(("grp", "step"), None),
        P(across, "step", None), P(across, "step", None),
    )
    return jax.shard_map(
        functools.partial(shards, sizes),
        mesh=mesh,
        in_specs=placed,
        out_specs=(P(across, "step", None), P("grp", None), P("grp")),
        check_vma=False,
    )
```

```python
import functools

import jax
import jax.numpy as jnp
from jax import lax
from jax.experimental import pallas as pl
from jax.experimental.pallas import tpu as pltpu
from jax.sharding import PartitionSpec as P

F32 = jnp.float32
BF16 = jnp.bfloat16
MESH = pl.DeviceIdType.MESH


def split(x):
    high = x.astype(BF16)
    return high, (x - high.astype(F32)).astype(BF16)


def rows_to_block(rows, steps, width):
    row = lax.broadcasted_iota(jnp.int32, (steps, width), 0)
    block = jnp.zeros((steps, width), F32)
    for t, value in rows.items():
        block = jnp.where(row == t, value, block)
    return block


def kernel(
    sizes, step_size,
    seed_ref, index_ref, init_hbm, noise_ref, weight_hbm, bias_hbm, rates_hbm, old_hbm, cot_hbm,
    path_ref, gw_ref, gb_ref,
    init_ref, weight_ref, bias_ref, rates_ref, old_ref, cot_ref, input_sem,
    noise_v, maps, off_cols, cot_cols, edge_in, fwd_in, bwd_in, fwd_out, bwd_out,
    all_prev, all_weighted, slope_v,
    noise_sem, edge_send, edge_recv, fwd_send, fwd_recv, bwd_send, bwd_recv,
    prev_send, prev_recv, weighted_send, weighted_recv,
):
    ranks, chains, reps = sizes
    peers = ranks * chains * reps
    steps, width = old_ref.shape
    half = width // 2
    s, c, r = lax.axis_index("step"), lax.axis_index("chain"), lax.axis_index("rep")
    me = (s * chains + c) * reps + r

    def peer(d):
        other = lax.rem(me + d, peers)
        return {
            "step": other // (chains * reps),
            "chain": lax.rem(other // reps, chains),
            "rep": lax.rem(other, reps),
        }

    def each_peer(body):
        if peers <= 32:
            for d in range(1, peers):
                body(d)
        else:
            def one(d, carry):
                body(d)
                return carry
            lax.fori_loop(1, peers, one, 0)

    inputs = [
        pltpu.make_async_copy(source, target, input_sem.at[k])
        for k, (source, target) in enumerate((
            (weight_hbm, weight_ref), (old_hbm, old_ref), (init_hbm, init_ref),
            (bias_hbm, bias_ref), (rates_hbm, rates_ref), (cot_hbm, cot_ref),
        ))
    ]
    for load in inputs:
        load.start()
    pieces = noise_sem.shape[0]
    piece = noise_ref.shape[0] // pieces
    loads = [
        pltpu.make_async_copy(
            noise_ref.at[pl.ds(k * piece, piece)], noise_v.at[pl.ds(k * piece, piece)], noise_sem.at[k]
        )
        for k in range(pieces)
    ]
    for load in loads:
        load.start()

    barrier = pltpu.get_barrier_semaphore()
    each_peer(
        lambda d: pl.semaphore_signal(barrier, inc=1, device_id=peer(d), device_id_type=MESH)
    )

    for load in inputs:
        load.wait()
    weight = weight_ref[...]
    weight_t = weight.T
    w_high, w_low = split(weight_t)
    pl.semaphore_wait(barrier, peers - 1)

    edge = pltpu.make_async_remote_copy(
        src_ref=old_ref.at[pl.ds(steps - 1, 1)], dst_ref=edge_in, send_sem=edge_send,
        recv_sem=edge_recv, device_id={"step": lax.rem(s + 1, ranks)}, device_id_type=MESH,
    )

    @pl.when(s < ranks - 1)
    def _():
        edge.start()

    start = init_ref[pl.ds(seed_ref[0], 1), :]
    for load in loads:
        load.wait()
    row = lax.broadcasted_iota(jnp.int32, (steps, width), 0)
    noise = jnp.concatenate([noise_v[pl.ds(index_ref[0, t], 1), :] for t in range(steps)], 0)

    @pl.when(s > 0)
    def _():
        edge.wait_recv()

    @pl.when(s == 0)
    def _():
        edge_in[...] = start

    first = edge_in[...]
    previous = jnp.concatenate([first, old_ref[0 : steps - 1, :]], 0)
    all_prev[0, 0] = previous

    plane = chains * reps
    mine = c * reps + r

    def along_step(data, sends, recvs, k):
        return pltpu.make_async_remote_copy(
            src_ref=data.at[0, 0], dst_ref=data.at[0, k], send_sem=sends.at[k],
            recv_sem=recvs.at[k],
            device_id={"step": lax.rem(s + k, ranks)}, device_id_type=MESH,
        )

    def in_plane(data, sends, recvs, d, k):
        other = lax.rem(mine + d, plane)
        return pltpu.make_async_remote_copy(
            src_ref=data.at[0, k], dst_ref=data.at[d, k], send_sem=sends.at[d * ranks + k],
            recv_sem=recvs.at[d * ranks + k],
            device_id={"chain": other // reps, "rep": lax.rem(other, reps)}, device_id_type=MESH,
        )

    def send_own(group):
        for k in range(1, ranks):
            along_step(*group, k).start()
        for d in range(1, plane):
            in_plane(*group, d, 0).start()

    def forward_block(group, k):
        along_step(*group, k).wait_recv()
        for d in range(1, plane):
            in_plane(*group, d, k).start()

    def forward_all(group):
        for q in reversed(range(ranks)):
            @pl.when(s != q)
            def _():
                forward_block(group, lax.rem(s - q + ranks, ranks))

    def wait_plane(group):
        for d in range(1, plane):
            for k in range(ranks):
                in_plane(*group, d, k).wait_recv()

    def wait_sent(group):
        for k in range(1, ranks):
            along_step(*group, k).wait_send()
        for d in range(1, plane):
            for k in range(ranks):
                in_plane(*group, d, k).wait_send()

    prev_group = (all_prev, prev_send, prev_recv)
    weighted_group = (all_weighted, weighted_send, weighted_recv)

    def dot(a, b):
        return jnp.dot(a, b, preferred_element_type=F32)

    p_high, p_low = split(previous)
    mixed = dot(p_high, w_high) + (dot(p_low, w_high) + dot(p_high, w_low))
    squash = jnp.tanh(mixed + bias_ref[...] + noise)
    slope = 1.0 - squash * squash
    slope_v[...] = slope
    offset = step_size * (squash - slope * mixed)
    scaled = step_size * slope
    keep = 1.0 - rates_ref[...]
    cot = cot_ref[...]
    stacked = jnp.concatenate([scaled, offset, cot, jnp.zeros((128 - 3 * steps, width), F32)], 0)
    columns = stacked.T
    lane = lax.broadcasted_iota(jnp.int32, (width, 128), 1)
    diagonal = lax.broadcasted_iota(jnp.int32, (width, width), 0) == lax.broadcasted_iota(
        jnp.int32, (width, width), 1
    )
    for t in range(steps):
        kept = jnp.where(diagonal, keep[t : t + 1], 0.0)
        if t % 2 == 0:
            maps[t] = weight * columns[:, t : t + 1] + kept
            off_cols[t // 2] = jnp.where(lane == steps + t, columns, 0.0)
            cot_cols[t // 2] = jnp.where(lane == 2 * steps + t, columns, 0.0)
        else:
            maps[t] = weight_t * scaled[t : t + 1] + kept

    def to_column(t, x, extra):
        part = maps[t, :, :half] * x[:, :half] + maps[t, :, half:] * x[:, half:]
        return jnp.sum(part + extra, axis=1, keepdims=True)

    def to_row(t, x):
        return jnp.sum(maps[t] * x, axis=0, keepdims=True)

    def gather_columns(cols):
        total = jnp.zeros((width, 128), F32)
        for t, value in cols.items():
            total = jnp.where(lane == t, value, total)
        return total.T[0:steps]

    forward = pltpu.make_async_remote_copy(
        src_ref=fwd_out, dst_ref=fwd_in, send_sem=fwd_send, recv_sem=fwd_recv,
        device_id={"step": lax.rem(s + 1, ranks)}, device_id_type=MESH,
    )
    backward = pltpu.make_async_remote_copy(
        src_ref=bwd_out, dst_ref=bwd_in, send_sem=bwd_send, recv_sem=bwd_recv,
        device_id={"step": lax.rem(s + ranks - 1, ranks)}, device_id_type=MESH,
    )

    def run_forward():
        @pl.when(s == 0)
        def _():
            fwd_in[...] = start

        @pl.when(s > 0)
        def _():
            forward.wait_recv()

        x = fwd_in[...]
        rows, cols = {}, {}
        for t in range(steps):
            if t % 2 == 0:
                x = to_column(t, x, off_cols[t // 2])
                cols[t] = x
            else:
                x = to_row(t, x) + offset[t : t + 1]
                rows[t] = x
        fwd_out[...] = x

        @pl.when(s < ranks - 1)
        def _():
            forward.start()

        path_ref[...] = jnp.where(
            row % 2 == 0, gather_columns(cols), rows_to_block(rows, steps, width)
        )

    def run_backward():
        @pl.when(s == ranks - 1)
        def _():
            bwd_in[...] = jnp.zeros((1, width), F32)

        @pl.when(s < ranks - 1)
        def _():
            backward.wait_recv()

        a = bwd_in[...] + cot[steps - 1 : steps]
        rows, cols = {steps - 1: a}, {}
        for t in range(steps - 1, 0, -1):
            if t % 2 == 1:
                a = to_column(t, a, cot_cols[(t - 1) // 2])
                cols[t - 1] = a
            else:
                a = to_row(t, a) + cot[t - 1 : t]
                rows[t - 1] = a
        bwd_out[...] = to_row(0, a)

        @pl.when(s > 0)
        def _():
            backward.start()

        adjoint = jnp.where(
            row % 2 == 0, gather_columns(cols), rows_to_block(rows, steps, width)
        )
        all_weighted[0, 0] = adjoint * slope_v[...]
        send_own(weighted_group)

    early = s < ranks // 2

    @pl.when(early)
    def _():
        run_forward()
        send_own(prev_group)
        run_backward()

    @pl.when(jnp.logical_not(early))
    def _():
        run_backward()
        send_own(prev_group)
        run_forward()

    forward_all(prev_group)
    wait_plane(prev_group)
    left = all_prev[...].reshape(peers * steps, width)
    l_high, l_low = split(left)
    forward_all(weighted_group)
    wait_plane(weighted_group)
    total = all_weighted[...].reshape(peers * steps, width)
    t_high, t_low = split(total)
    dims = (((0,), (0,)), ((), ()))

    def outer(a, b):
        return lax.dot_general(a, b, dims, preferred_element_type=F32)

    gw_ref[...] = step_size * (
        outer(t_high, l_high) + (outer(t_low, l_high) + outer(t_high, l_low))
    )
    gb_ref[...] = step_size * jnp.sum(total, axis=0, keepdims=True)

    wait_sent(prev_group)
    wait_sent(weighted_group)

    @pl.when(s < ranks - 1)
    def _():
        edge.wait_send()
        forward.wait_send()

    @pl.when(s > 0)
    def _():
        backward.wait_send()


def shards(sizes, seed, index, init_table, noise_table, weight, bias, rates, old_path, cotangent):
    ranks, chains, reps = sizes
    peers = ranks * chains * reps
    _, steps, width = old_path.shape
    vmem = pl.BlockSpec(memory_space=pltpu.VMEM)
    smem = pl.BlockSpec(memory_space=pltpu.SMEM)
    dma = pltpu.SemaphoreType.DMA
    path, grad_w, grad_b = pl.pallas_call(
        functools.partial(kernel, sizes, 4.0 / (steps * ranks)),
        out_shape=(
            jax.ShapeDtypeStruct((steps, width), F32),
            jax.ShapeDtypeStruct((width, width), F32),
            jax.ShapeDtypeStruct((1, width), F32),
        ),
        in_specs=[smem, smem] + [pl.BlockSpec(memory_space=pltpu.HBM)] * 7,
        out_specs=(vmem, vmem, vmem),
        scratch_shapes=[
            pltpu.VMEM(init_table.shape, F32),
            pltpu.VMEM(weight.shape, F32),
            pltpu.VMEM((1, width), F32),
            pltpu.VMEM(rates.shape, F32),
            pltpu.VMEM((steps, width), F32),
            pltpu.VMEM((steps, width), F32),
            dma((6,)),
            pltpu.VMEM(noise_table.shape, F32),
            pltpu.VMEM((steps, width, width), F32),
            pltpu.VMEM((steps // 2, width, 128), F32),
            pltpu.VMEM((steps // 2, width, 128), F32),
            pltpu.VMEM((1, width), F32),
            pltpu.VMEM((1, width), F32),
            pltpu.VMEM((1, width), F32),
            pltpu.VMEM((1, width), F32),
            pltpu.VMEM((1, width), F32),
            pltpu.VMEM((chains * reps, ranks, steps, width), F32),
            pltpu.VMEM((chains * reps, ranks, steps, width), F32),
            pltpu.VMEM((steps, width), F32),
            dma((8,)),
            dma, dma, dma, dma, dma, dma,
            dma((peers,)), dma((peers,)), dma((peers,)), dma((peers,)),
        ],
        compiler_params=pltpu.CompilerParams(
            collective_id=0, has_side_effects=True, vmem_limit_bytes=64 * 1024 * 1024 - 4096
        ),
    )(
        seed, index, init_table, noise_table, weight, bias.reshape(1, width), rates,
        old_path.reshape(steps, width), cotangent.reshape(steps, width),
    )
    return path.reshape(1, steps, width), grad_w, grad_b.reshape(width)


def solution(mesh):
    sizes = (mesh.shape["step"], mesh.shape["chain"], mesh.shape["rep"])
    across = ("grp", "chain", "rep")
    placed = (
        P(across), P(across, "step"), P(), P(), P(), P(), P(("grp", "step"), None),
        P(across, "step", None), P(across, "step", None),
    )
    return jax.shard_map(
        functools.partial(shards, sizes),
        mesh=mesh,
        in_specs=placed,
        out_specs=(P(across, "step", None), P("grp", None), P("grp")),
        check_vma=False,
    )
```

```python
import functools

import jax
import jax.numpy as jnp
from jax import lax
from jax.experimental import pallas as pl
from jax.experimental.pallas import tpu as pltpu
from jax.sharding import PartitionSpec as P

F32 = jnp.float32
BF16 = jnp.bfloat16
MESH = pl.DeviceIdType.MESH


def split(x):
    high = x.astype(BF16)
    return high, (x - high.astype(F32)).astype(BF16)


def rows_to_block(rows, steps, width):
    row = lax.broadcasted_iota(jnp.int32, (steps, width), 0)
    block = jnp.zeros((steps, width), F32)
    for t, value in rows.items():
        block = jnp.where(row == t, value, block)
    return block


def kernel(
    sizes, step_size,
    seed_ref, index_ref, init_hbm, noise_ref, weight_hbm, bias_hbm, rates_hbm, old_hbm, cot_hbm,
    path_ref, gw_ref, gb_ref,
    init_ref, weight_ref, bias_ref, rates_ref, old_ref, cot_ref, input_sem,
    noise_v, maps, off_cols, cot_cols, edge_in, fwd_in, bwd_in, fwd_out, bwd_out,
    all_prev, all_weighted, slope_v,
    noise_sem, edge_send, edge_recv, fwd_send, fwd_recv, bwd_send, bwd_recv,
    prev_send, prev_recv, weighted_send, weighted_recv,
):
    ranks, chains, reps = sizes
    peers = ranks * chains * reps
    steps, width = old_ref.shape
    half = width // 2
    s, c, r = lax.axis_index("step"), lax.axis_index("chain"), lax.axis_index("rep")

    def wrap(x, size):
        return jnp.where(x >= size, x - size, x)

    def peer(d):
        return {
            "step": wrap(s + d // (chains * reps), ranks),
            "chain": wrap(c + d // reps % chains, chains),
            "rep": wrap(r + d % reps, reps),
        }

    def each_peer(body):
        if peers <= 32:
            for d in range(1, peers):
                body(d)
        else:
            def one(d, carry):
                body(d)
                return carry
            lax.fori_loop(1, peers, one, 0)

    inputs = [
        pltpu.make_async_copy(source, target, input_sem.at[k])
        for k, (source, target) in enumerate((
            (weight_hbm, weight_ref), (old_hbm, old_ref), (init_hbm, init_ref),
            (bias_hbm, bias_ref), (rates_hbm, rates_ref), (cot_hbm, cot_ref),
        ))
    ]
    for load in inputs:
        load.start()
    pieces = noise_sem.shape[0]
    piece = noise_ref.shape[0] // pieces
    loads = [
        pltpu.make_async_copy(
            noise_ref.at[pl.ds(k * piece, piece)], noise_v.at[pl.ds(k * piece, piece)], noise_sem.at[k]
        )
        for k in range(pieces)
    ]
    for load in loads:
        load.start()

    barrier = pltpu.get_barrier_semaphore()
    each_peer(
        lambda d: pl.semaphore_signal(barrier, inc=1, device_id=peer(d), device_id_type=MESH)
    )

    for load in inputs:
        load.wait()
    weight = weight_ref[...]
    weight_t = weight.T
    w_high, w_low = split(weight_t)
    pl.semaphore_wait(barrier, peers - 1)

    edge = pltpu.make_async_remote_copy(
        src_ref=old_ref.at[pl.ds(steps - 1, 1)], dst_ref=edge_in, send_sem=edge_send,
        recv_sem=edge_recv, device_id={"step": lax.rem(s + 1, ranks)}, device_id_type=MESH,
    )

    @pl.when(s < ranks - 1)
    def _():
        edge.start()

    start = init_ref[pl.ds(seed_ref[0], 1), :]
    for load in loads:
        load.wait()
    row = lax.broadcasted_iota(jnp.int32, (steps, width), 0)
    noise = jnp.concatenate([noise_v[pl.ds(index_ref[0, t], 1), :] for t in range(steps)], 0)

    @pl.when(s > 0)
    def _():
        edge.wait_recv()

    @pl.when(s == 0)
    def _():
        edge_in[...] = start

    first = edge_in[...]
    previous = jnp.concatenate([first, old_ref[0 : steps - 1, :]], 0)
    all_prev[0] = previous

    def prev_copy(d):
        return pltpu.make_async_remote_copy(
            src_ref=all_prev.at[0], dst_ref=all_prev.at[d], send_sem=prev_send.at[d],
            recv_sem=prev_recv.at[d], device_id=peer(d), device_id_type=MESH,
        )

    def weighted_copy(d):
        return pltpu.make_async_remote_copy(
            src_ref=all_weighted.at[0], dst_ref=all_weighted.at[d], send_sem=weighted_send.at[d],
            recv_sem=weighted_recv.at[d], device_id=peer(d), device_id_type=MESH,
        )

    def dot(a, b):
        return jnp.dot(a, b, preferred_element_type=F32)

    p_high, p_low = split(previous)
    mixed = dot(p_high, w_high) + (dot(p_low, w_high) + dot(p_high, w_low))
    squash = jnp.tanh(mixed + bias_ref[...] + noise)
    slope = 1.0 - squash * squash
    slope_v[...] = slope
    offset = step_size * (squash - slope * mixed)
    scaled = step_size * slope
    keep = 1.0 - rates_ref[...]
    cot = cot_ref[...]
    stacked = jnp.concatenate([scaled, offset, cot, jnp.zeros((128 - 3 * steps, width), F32)], 0)
    columns = stacked.T
    lane = lax.broadcasted_iota(jnp.int32, (width, 128), 1)
    diagonal = lax.broadcasted_iota(jnp.int32, (width, width), 0) == lax.broadcasted_iota(
        jnp.int32, (width, width), 1
    )
    for t in range(steps):
        kept = jnp.where(diagonal, keep[t : t + 1], 0.0)
        if t % 2 == 0:
            maps[t] = weight * columns[:, t : t + 1] + kept
            off_cols[t // 2] = jnp.where(lane == steps + t, columns, 0.0)
            cot_cols[t // 2] = jnp.where(lane == 2 * steps + t, columns, 0.0)
        else:
            maps[t] = weight_t * scaled[t : t + 1] + kept

    def to_column(t, x, extra):
        part = maps[t, :, :half] * x[:, :half] + maps[t, :, half:] * x[:, half:]
        return jnp.sum(part + extra, axis=1, keepdims=True)

    def to_row(t, x):
        return jnp.sum(maps[t] * x, axis=0, keepdims=True)

    def gather_columns(cols):
        total = jnp.zeros((width, 128), F32)
        for t, value in cols.items():
            total = jnp.where(lane == t, value, total)
        return total.T[0:steps]

    forward = pltpu.make_async_remote_copy(
        src_ref=fwd_out, dst_ref=fwd_in, send_sem=fwd_send, recv_sem=fwd_recv,
        device_id={"step": lax.rem(s + 1, ranks)}, device_id_type=MESH,
    )
    backward = pltpu.make_async_remote_copy(
        src_ref=bwd_out, dst_ref=bwd_in, send_sem=bwd_send, recv_sem=bwd_recv,
        device_id={"step": lax.rem(s + ranks - 1, ranks)}, device_id_type=MESH,
    )

    def run_forward():
        @pl.when(s == 0)
        def _():
            fwd_in[...] = start

        @pl.when(s > 0)
        def _():
            forward.wait_recv()

        x = fwd_in[...]
        rows, cols = {}, {}
        for t in range(steps):
            if t % 2 == 0:
                x = to_column(t, x, off_cols[t // 2])
                cols[t] = x
            else:
                x = to_row(t, x) + offset[t : t + 1]
                rows[t] = x
        fwd_out[...] = x

        @pl.when(s < ranks - 1)
        def _():
            forward.start()

        path_ref[...] = jnp.where(
            row % 2 == 0, gather_columns(cols), rows_to_block(rows, steps, width)
        )

    def run_backward():
        @pl.when(s == ranks - 1)
        def _():
            bwd_in[...] = jnp.zeros((1, width), F32)

        @pl.when(s < ranks - 1)
        def _():
            backward.wait_recv()

        a = bwd_in[...] + cot[steps - 1 : steps]
        rows, cols = {steps - 1: a}, {}
        for t in range(steps - 1, 0, -1):
            if t % 2 == 1:
                a = to_column(t, a, cot_cols[(t - 1) // 2])
                cols[t - 1] = a
            else:
                a = to_row(t, a) + cot[t - 1 : t]
                rows[t - 1] = a
        bwd_out[...] = to_row(0, a)

        @pl.when(s > 0)
        def _():
            backward.start()

        adjoint = jnp.where(
            row % 2 == 0, gather_columns(cols), rows_to_block(rows, steps, width)
        )
        all_weighted[0] = adjoint * slope_v[...]
        each_peer(lambda d: weighted_copy(d).start())

    early = s < ranks // 2

    @pl.when(early)
    def _():
        run_forward()
        each_peer(lambda d: prev_copy(d).start())
        run_backward()

    @pl.when(jnp.logical_not(early))
    def _():
        run_backward()
        each_peer(lambda d: prev_copy(d).start())
        run_forward()

    each_peer(lambda d: prev_copy(d).wait_recv())
    left = all_prev[...].reshape(peers * steps, width)
    l_high, l_low = split(left)
    each_peer(lambda d: weighted_copy(d).wait_recv())
    total = all_weighted[...].reshape(peers * steps, width)
    t_high, t_low = split(total)
    dims = (((0,), (0,)), ((), ()))

    def outer(a, b):
        return lax.dot_general(a, b, dims, preferred_element_type=F32)

    gw_ref[...] = step_size * (
        outer(t_high, l_high) + (outer(t_low, l_high) + outer(t_high, l_low))
    )
    gb_ref[...] = step_size * jnp.sum(total, axis=0, keepdims=True)

    each_peer(lambda d: prev_copy(d).wait_send())
    each_peer(lambda d: weighted_copy(d).wait_send())

    @pl.when(s < ranks - 1)
    def _():
        edge.wait_send()
        forward.wait_send()

    @pl.when(s > 0)
    def _():
        backward.wait_send()


def shards(sizes, seed, index, init_table, noise_table, weight, bias, rates, old_path, cotangent):
    ranks, chains, reps = sizes
    peers = ranks * chains * reps
    _, steps, width = old_path.shape
    vmem = pl.BlockSpec(memory_space=pltpu.VMEM)
    smem = pl.BlockSpec(memory_space=pltpu.SMEM)
    dma = pltpu.SemaphoreType.DMA
    path, grad_w, grad_b = pl.pallas_call(
        functools.partial(kernel, sizes, 4.0 / (steps * ranks)),
        out_shape=(
            jax.ShapeDtypeStruct((steps, width), F32),
            jax.ShapeDtypeStruct((width, width), F32),
            jax.ShapeDtypeStruct((1, width), F32),
        ),
        in_specs=[smem, smem] + [pl.BlockSpec(memory_space=pltpu.HBM)] * 7,
        out_specs=(vmem, vmem, vmem),
        scratch_shapes=[
            pltpu.VMEM(init_table.shape, F32),
            pltpu.VMEM(weight.shape, F32),
            pltpu.VMEM((1, width), F32),
            pltpu.VMEM(rates.shape, F32),
            pltpu.VMEM((steps, width), F32),
            pltpu.VMEM((steps, width), F32),
            dma((6,)),
            pltpu.VMEM(noise_table.shape, F32),
            pltpu.VMEM((steps, width, width), F32),
            pltpu.VMEM((steps // 2, width, 128), F32),
            pltpu.VMEM((steps // 2, width, 128), F32),
            pltpu.VMEM((1, width), F32),
            pltpu.VMEM((1, width), F32),
            pltpu.VMEM((1, width), F32),
            pltpu.VMEM((1, width), F32),
            pltpu.VMEM((1, width), F32),
            pltpu.VMEM((peers, steps, width), F32),
            pltpu.VMEM((peers, steps, width), F32),
            pltpu.VMEM((steps, width), F32),
            dma((8,)),
            dma, dma, dma, dma, dma, dma,
            dma((peers,)), dma((peers,)), dma((peers,)), dma((peers,)),
        ],
        compiler_params=pltpu.CompilerParams(
            collective_id=0, has_side_effects=True, vmem_limit_bytes=64 * 1024 * 1024 - 4096
        ),
    )(
        seed, index, init_table, noise_table, weight, bias.reshape(1, width), rates,
        old_path.reshape(steps, width), cotangent.reshape(steps, width),
    )
    return path.reshape(1, steps, width), grad_w, grad_b.reshape(width)


def solution(mesh):
    sizes = (mesh.shape["step"], mesh.shape["chain"], mesh.shape["rep"])
    across = ("grp", "chain", "rep")
    placed = (
        P(across), P(across, "step"), P(), P(), P(), P(), P(("grp", "step"), None),
        P(across, "step", None), P(across, "step", None),
    )
    return jax.shard_map(
        functools.partial(shards, sizes),
        mesh=mesh,
        in_specs=placed,
        out_specs=(P(across, "step", None), P("grp", None), P("grp")),
        check_vma=False,
    )
```
